32 devices in a mesh: row: 4 (over x, core), circ: 8 (over z, y).
Axes of the slice: x: 2, y: 2, z: 4, core: 2. Of those that a mesh axis runs over, the one named last changes fastest.
Arguments:
- flow_state: float32 [5, 64, 32, 1024], P(None, 'row', None, 'circ'), may hold values from -4 to 4
- velocity: float32 [3, 64, 32, 1024], P(None, 'row', None, 'circ'), may hold values from -3 to 3
- offsets: int32 [3, 3], replicated, may hold values from 0 to 1023, as said below
- passage_shift: int32 [4], replicated, may hold values from 0 to 7, as said below
- donor_step: int32 [4, 2, 1024], P('row', None, 'circ'), may hold values from 0 to 127
- donor_weight: float32 [4, 2, 1024], P('row', None, 'circ'), may hold values from 0.05 to 0.95
Outputs:
- updated_state: float32 [5, 64, 32, 1024], P(None, 'row', None, 'circ')
The draws below stay inside these ranges and needn't reach their ends.
Inputs may be any that keep to these rules, and one draw needn't show every extreme that they name: Rotation offsets in cells; some interface takes the offset 1024 - 1 at some section in every draw, and with two or more interfaces some takes 0. `passage_shift`: passage index placed on device column 0 of each row; some row has 8 - 1 and some row 0 in every draw.
All inputs are finite; a program needn't handle non-finite values.
Results may differ from the reference program's by a relative error of at most 0.0003.
Values sent between devices are 32-bit elements; how exact they have to be, the bound alone decides.
A program may use at most 128 MiB of HBM per device.

```python
import jax
import jax.numpy as jnp
from jax import lax

AX = 16
RA = 32
CC = 128
SECTIONS = 3
COMPS = 5
ROWS = 4
IFACES = 3
PASSAGES = 8
AXIAL = 64
NC = 1024


def joint_draw(key):
    base = jax.random.fold_in(key, 4711)
    key_shift = jax.random.fold_in(base, 1)
    key_offs = jax.random.fold_in(base, 2)
    key_part = jax.random.fold_in(base, 3)
    key_near = jax.random.fold_in(base, 5)
    shifts = jax.random.randint(key_shift, (ROWS,), 0, PASSAGES, dtype=jnp.int32)
    row_ids = jnp.arange(ROWS, dtype=jnp.int32)
    shifts = jnp.where(row_ids == 0, PASSAGES - 1, shifts)
    shifts = jnp.where(row_ids == ROWS - 1, 0, shifts)
    offs = jax.random.randint(key_offs, (SECTIONS, IFACES), 0, NC, dtype=jnp.int32)
    within = jax.random.randint(key_part, (IFACES,), 0, CC, dtype=jnp.int32)
    near_within = jax.random.randint(key_near, (IFACES,), 0, CC, dtype=jnp.int32)
    forced = (PASSAGES // 2 - shifts[:-1] + shifts[1:]) % PASSAGES * CC + within
    behind = (shifts[1:] - shifts[:-1] - 1) % PASSAGES * CC + near_within
    section_row = jnp.arange(SECTIONS, dtype=jnp.int32)[:, None]
    face_col = jnp.arange(IFACES, dtype=jnp.int32)[None, :]
    offs = jnp.where(section_row == 0, forced[None, :], offs)
    offs = jnp.where(section_row == 1, behind[None, :], offs)
    offs = jnp.where((section_row == 2) & (face_col == 0), NC - 1, offs)
    if IFACES > 1:
        offs = jnp.where((section_row == 2) & (face_col == IFACES - 1), 0, offs)
    return (shifts, offs)


def draw_offsets(key, part):
    return joint_draw(key)[1]


def draw_passage_shift(key, part):
    return joint_draw(key)[0]


def place_ends(entries, rng, low, largest):
    index_at = [jax.random.randint(jax.random.fold_in(rng, axis), (), 0, length) for axis, length in enumerate(entries.shape)]
    longest = entries.shape.index(max(entries.shape))
    neighbour = index_at[:longest] + [(index_at[longest] + 1) % entries.shape[longest]] + index_at[longest + 1:]
    return entries.at[tuple(index_at)].set(low).at[tuple(neighbour)].set(largest)


def block_levels(own_key, extent, pieces, low, high):
    loudness = 1.0
    for dim, parts in pieces:
        draws = jax.random.uniform(jax.random.fold_in(jax.random.fold_in(own_key, 6), dim), (parts,), jnp.float32, low / len(pieces), high / len(pieces))
        loudness = loudness * jnp.repeat(jnp.exp(draws), extent[dim] // parts).reshape((-1,) + (1,) * (len(extent) - 1 - dim))
    return loudness


def noise(rng, shape, scale, bound, cuts=(), kind=jnp.bfloat16):
    loudness = block_levels(rng, shape, cuts, -0.22, 0.18) if cuts else 1.0
    values = jax.random.normal(rng, shape, jnp.float32) * scale * loudness
    return jnp.minimum(jnp.maximum(values, -bound), bound).astype(kind)


def setup_inputs(seed: int = 0) -> dict:
    seeds = jax.random.split(jax.random.key(seed), 7)
    return {
        "flow_state": noise(seeds[0], (COMPS, AXIAL, RA, NC), 1.0, 4.0, ((1, 4), (3, 8)), jnp.float32),
        "velocity": noise(seeds[1], (3, AXIAL, RA, NC), 0.6, 3.0, ((1, 4), (3, 8)), jnp.float32),
        "offsets": draw_offsets(jax.random.fold_in(seeds[6], 71), 0),
        "passage_shift": draw_passage_shift(jax.random.fold_in(seeds[6], 71), 0),
        "donor_step": place_ends(jax.random.randint(seeds[4], (ROWS, 2, NC), 0, CC), jax.random.fold_in(seeds[4], 1), 0, CC - 1).astype(jnp.int32),
        "donor_weight": jnp.clip(0.05 + 0.9 * jax.random.uniform(seeds[5], (ROWS, 2, NC), jnp.float32) ** block_levels(seeds[5], (ROWS, 2, NC), ((0, 4), (2, 8)), -0.2, 0.2), 0.05, 0.95),
    }


SMAG_COEF = 0.1
TIME_STEP = 0.25

def combine(fields, axial_ext, radial_ext, around_ext, velocity):
    d_axial = 0.5 * (axial_ext[:, 2:] - axial_ext[:, :-2])
    d_radial = 0.5 * (radial_ext[:, :, 2:] - radial_ext[:, :, :-2])
    d_around = 0.5 * (around_ext[..., 2:] - around_ext[..., :-2])
    laplace = axial_ext[:, 2:] + axial_ext[:, :-2] + radial_ext[:, :, 2:] + radial_ext[:, :, :-2] + around_ext[..., 2:] + around_ext[..., :-2] - 6.0 * fields
    strain = lax.optimization_barrier(jnp.sum(d_axial[1:4] ** 2 + d_radial[1:4] ** 2 + d_around[1:4] ** 2, axis=0))
    eddy_visc = SMAG_COEF * jnp.sqrt(strain + 1.0)
    return eddy_visc * laplace - (velocity[0] * d_axial + velocity[1] * d_radial + velocity[2] * d_around)

def radial_pad(fields):
    return jnp.concatenate([fields[:, :, :1], fields, fields[:, :, -1:]], axis=2)

def axial_pad(fields, lower_ghost, upper_ghost):
    return jnp.concatenate([lower_ghost[:, None], fields, upper_ghost[:, None]], axis=1)

def ghost_plane(source, donor_steps, weights, offset, loop_cells):
    donor_cols = (jnp.arange(loop_cells, dtype=jnp.int32) + offset + donor_steps) % loop_cells
    next_cols = (donor_cols + 1) % loop_cells
    return weights * source[:, :, donor_cols] + (1.0 - weights) * source[:, :, next_cols]

def reference(flow_state, velocity, offsets, passage_shift, donor_step, donor_weight):
    loop_cells = flow_state.shape[-1]

    def ordered(values, row_index):
        return jnp.roll(values, -passage_shift[row_index] * CC, axis=-1)
    start_rows = [ordered(flow_state[:, row_index * AX:(row_index + 1) * AX], row_index) for row_index in range(ROWS)]
    speeds = [ordered(velocity[:, row_index * AX:(row_index + 1) * AX], row_index) for row_index in range(ROWS)]
    donor_cols = [ordered(donor_step[row_index], row_index) for row_index in range(ROWS)]
    donor_wts = [ordered(donor_weight[row_index], row_index) for row_index in range(ROWS)]

    def evaluate(fields_list, section_index):
        result = []
        for row_index in range(ROWS):
            fields = fields_list[row_index]
            if row_index > 0:
                lower_ghost = ghost_plane(fields_list[row_index - 1][:, -1], donor_cols[row_index][0], donor_wts[row_index][0], offsets[section_index, row_index - 1], loop_cells)
            else:
                lower_ghost = fields[:, 0]
            if row_index < ROWS - 1:
                upper_ghost = ghost_plane(fields_list[row_index + 1][:, 0], donor_cols[row_index][1], donor_wts[row_index][1], -offsets[section_index, row_index], loop_cells)
            else:
                upper_ghost = fields[:, -1]
            around_ext = jnp.concatenate([fields[..., -1:], fields, fields[..., :1]], axis=3)
            result.append(combine(fields, axial_pad(fields, lower_ghost, upper_ghost), radial_pad(fields), around_ext, speeds[row_index]))
        return result
    first_rate = evaluate(start_rows, 0)
    section_one = [start_rows[row_index] + TIME_STEP * first_rate[row_index] for row_index in range(ROWS)]
    second_rate = evaluate(section_one, 1)
    section_two = [0.75 * start_rows[row_index] + 0.25 * (section_one[row_index] + TIME_STEP * second_rate[row_index]) for row_index in range(ROWS)]
    third_rate = evaluate(section_two, 2)
    section_three = [1.0 / 3.0 * start_rows[row_index] + 2.0 / 3.0 * (section_two[row_index] + TIME_STEP * third_rate[row_index]) for row_index in range(ROWS)]
    restored = [jnp.roll(section_three[row_index], passage_shift[row_index] * CC, axis=-1) for row_index in range(ROWS)]
    return jnp.concatenate(restored, axis=1)
```

```python
import functools

import jax
import jax.numpy as jnp
from jax import lax
from jax.experimental import pallas as pl
from jax.experimental.pallas import tpu as pltpu
from jax.sharding import PartitionSpec as P

SMAG_COEF = 0.1
TIME_STEP = 0.25
SECTIONS = 3
LANES = 128
GROUP = 8


def kernel(
    row_count, count,
    q_ref, u_ref, off_ref, shift_ref, step_ref, weight_ref, out_ref,
    v1, v2, pack, halo, comb, sel, ghost,
    send_sem, fwd_sem, recv_sem, halo_send, halo_recv, *slots
):
    comps, planes, radial, cells = q_ref.shape
    groups = radial // GROUP
    half = count // 2
    loop_cells = count * cells
    row = lax.axis_index("row")
    col = lax.axis_index("circ")
    odd = lax.rem(col, 2)
    partner = col + 1 - 2 * odd
    right = lax.rem(col + 1, count)
    left = lax.rem(col + count - 1, count)
    has = (row > 0, row < row_count - 1)
    other_row = (row - 1, row + 1)
    fields = (q_ref, v1, v2, out_ref)
    order = sorted(range(half), key=lambda d: (min(d, half - d), d))

    lane = lax.broadcasted_iota(jnp.int32, (radial, cells), 1)
    line = lax.broadcasted_iota(jnp.int32, (radial, cells), 0)
    lane8 = lax.broadcasted_iota(jnp.int32, (GROUP, cells), 1)
    is_first, is_last = lane == 0, lane == cells - 1
    is_inner, is_outer = line == 0, line == radial - 1

    def away(d):
        return lax.rem(col + 2 * d, count)

    def back(d):
        return lax.rem(col + count - 2 * d, count)

    def across(d):
        return lax.rem(partner + count - 2 * d, count)

    def face_copy(s, face, d):
        plane = planes - 1 if face == 0 else 0
        return pltpu.make_async_remote_copy(
            src_ref=fields[s].at[:, plane],
            dst_ref=slots[2 * s + face].at[col],
            send_sem=send_sem.at[s, face, d],
            recv_sem=recv_sem.at[s, face, col],
            device_id={"row": other_row[1 - face], "circ": away(d)},
            device_id_type=pl.DeviceIdType.MESH,
        )

    def forward_copy(s, face, d):
        return pltpu.make_async_remote_copy(
            src_ref=slots[2 * s + face].at[back(d)],
            dst_ref=slots[2 * s + face].at[back(d)],
            send_sem=fwd_sem.at[s, face, d],
            recv_sem=recv_sem.at[s, face, back(d)],
            device_id={"row": row, "circ": partner},
            device_id_type=pl.DeviceIdType.MESH,
        )

    def arrival(s, face, slot):
        return pltpu.make_async_remote_copy(
            src_ref=slots[2 * s + face].at[slot],
            dst_ref=slots[2 * s + face].at[slot],
            send_sem=fwd_sem.at[s, face, 0],
            recv_sem=recv_sem.at[s, face, slot],
            device_id={"row": row, "circ": partner},
            device_id_type=pl.DeviceIdType.MESH,
        )

    def halo_copy(s, side):
        return pltpu.make_async_remote_copy(
            src_ref=pack.at[s],
            dst_ref=halo.at[s, side],
            send_sem=halo_send.at[s, side],
            recv_sem=halo_recv.at[s, side],
            device_id={"row": row, "circ": right if side == 0 else left},
            device_id_type=pl.DeviceIdType.MESH,
        )

    def send_face(s, face):
        @pl.when(has[1 - face])
        def _():
            for d in order:
                face_copy(s, face, d).start()

    def send_halo(s):
        halo_copy(s, 0).start()
        halo_copy(s, 1).start()

    def forward(s, d):
        for face in (0, 1):
            @pl.when(has[face])
            def _():
                arrival(s, face, back(d)).wait_recv()
                forward_copy(s, face, d).start()

    def put_ends(s, m, a, value):
        packed = pack[s, m]
        for g in range(groups):
            spot = 2 * (a * groups + g)
            here = jnp.bitwise_and(lane8 + 1 - spot, cells - 1) < 2
            moved = pltpu.roll(value[g * GROUP:(g + 1) * GROUP], spot, 1)
            packed = jnp.where(here, moved, packed)
        pack[s, m] = packed

    def donor_base(s, face):
        source = jnp.clip(other_row[face], 0, row_count - 1)
        at = jnp.clip(row - 1 + face, 0, row_count - 2)
        offset = off_ref[s, at]
        offset = offset if face == 0 else lax.rem(loop_cells - offset, loop_cells)
        passage = col - shift_ref[row] + shift_ref[source] + offset // cells + 2 * count
        return passage, lax.rem(offset, cells)

    def build_select(s):
        spots = lax.broadcasted_iota(jnp.int32, (3 * cells, cells), 0)
        within = lax.broadcasted_iota(jnp.int32, (1, cells), 1)
        for face in (0, 1):
            _, start = donor_base(s, face)
            donor = within + start + step_ref[0, face:face + 1, :]
            for nxt in (0, 1):
                hot = jnp.where(spots == donor + nxt, 1.0, 0.0).astype(jnp.bfloat16)
                sel[face, :, nxt * cells:(nxt + 1) * cells] = hot

    def make_ghost(s, face):
        @pl.when(has[face])
        def _():
            passage, _ = donor_base(s, face)
            total = None
            for k in range(3):
                block = slots[2 * s + face][lax.rem(passage + k, count)].reshape(comps * radial, cells)
                high = block.astype(jnp.bfloat16)
                low = (block - high.astype(jnp.float32)).astype(jnp.bfloat16)
                part = sel[face, k * cells:(k + 1) * cells, :]
                for piece in (high, low):
                    got = jnp.dot(piece, part, preferred_element_type=jnp.float32)
                    total = got if total is None else total + got
            weight = weight_ref[0, face:face + 1, :]
            value = weight * total[:, :cells] + (1.0 - weight) * total[:, cells:]
            ghost[face] = value.reshape(comps, radial, cells)

        @pl.when(jnp.logical_not(has[face]))
        def _():
            ghost[face] = fields[s][:, 0 if face == 0 else planes - 1]

    def update(s, a, lower, upper):
        src, dst = fields[s], fields[s + 1]
        u_ax, u_rad, u_circ = 0.5 * u_ref[0, a], 0.5 * u_ref[1, a], 0.5 * u_ref[2, a]

        def terms(m):
            v, lo, hi = src[m, a], lower(m), upper(m)
            inner = jnp.where(is_inner, v, pltpu.roll(v, 1, 0))
            outer = jnp.where(is_outer, v, pltpu.roll(v, radial - 1, 0))
            edge = comb[m]
            ends = jnp.concatenate(
                [
                    pltpu.roll(edge, jnp.bitwise_and(2 * cells - 2 * (a * groups + g), cells - 1), 1)
                    for g in range(groups)
                ],
                axis=0,
            )
            before = pltpu.roll(jnp.where(is_last, ends, v), 1, 1)
            after = pltpu.roll(jnp.where(is_first, ends, v), cells - 1, 1)
            d_ax, d_rad, d_circ = hi - lo, outer - inner, after - before
            lap = ((hi + lo) + (outer + inner)) + ((after + before) - 6.0 * v)
            adv = u_ax * d_ax + u_rad * d_rad + u_circ * d_circ
            return v, d_ax, d_rad, d_circ, lap, adv

        def finish(m, v, lap, adv, nu):
            rate = nu * lap - adv
            if s == 0:
                new = v + TIME_STEP * rate
            elif s == 1:
                new = 0.75 * q_ref[m, a] + 0.25 * (v + TIME_STEP * rate)
            else:
                new = (1.0 / 3.0) * q_ref[m, a] + (2.0 / 3.0) * (v + TIME_STEP * rate)
            dst[m, a] = new
            if s + 1 < SECTIONS:
                put_ends(s + 1, m, a, new)

        strain = jnp.zeros((radial, cells), jnp.float32)
        held = []
        for m in (1, 2, 3):
            v, d_ax, d_rad, d_circ, lap, adv = terms(m)
            strain = strain + (d_ax * d_ax + d_rad * d_rad + d_circ * d_circ)
            held.append((m, v, lap, adv))
        nu = SMAG_COEF * jnp.sqrt(0.25 * strain + 1.0)
        for m, v, lap, adv in held:
            finish(m, v, lap, adv, nu)
        for m in (0, *range(4, comps)):
            v, _, _, _, lap, adv = terms(m)
            finish(m, v, lap, adv, nu)

    def inside(s, first, last):
        src = fields[s]

        def body(a, carry):
            update(s, a, lambda m: src[m, a - 1], lambda m: src[m, a + 1])
            return carry

        lax.fori_loop(first, last, body, 0)

    barrier = pltpu.get_barrier_semaphore()
    for side in (left, right):
        pl.semaphore_signal(
            barrier, inc=1, device_id={"row": row, "circ": side}, device_id_type=pl.DeviceIdType.MESH
        )
    for face in (0, 1):
        @pl.when(has[face])
        def _():
            for d in range(half):
                pl.semaphore_signal(
                    barrier, inc=1, device_id={"row": other_row[face], "circ": away(d)},
                    device_id_type=pl.DeviceIdType.MESH,
                )

    pack[...] = jnp.zeros_like(pack)

    def first_ends(a, carry):
        for m in range(comps):
            put_ends(0, m, a, q_ref[m, a])
        return carry

    lax.fori_loop(0, planes, first_ends, 0)
    pl.semaphore_wait(barrier, 2 + half * (has[0].astype(jnp.int32) + has[1].astype(jnp.int32)))

    cuts = [1 + (planes - 2) * i // half for i in range(half + 1)]
    for s in range(SECTIONS):
        src = fields[s]
        if s == 0:
            send_face(s, 0)
            send_face(s, 1)
        send_halo(s)
        build_select(s)
        for side in (0, 1):
            halo_copy(s, side).wait_recv()
        for m in range(comps):
            comb[m] = jnp.where(jnp.bitwise_and(lane8, 1) == 0, halo[s, 1, m], halo[s, 0, m])
        for i, d in enumerate(order):
            forward(s, d)
            if cuts[i] < cuts[i + 1]:
                inside(s, cuts[i], cuts[i + 1])
        for face in (0, 1):
            @pl.when(has[face])
            def _():
                for d in order:
                    arrival(s, face, across(d)).wait_recv()
            make_ghost(s, face)
            if face == 0:
                update(s, 0, lambda m: ghost[0, m], lambda m: src[m, 1])
            else:
                update(s, planes - 1, lambda m: src[m, planes - 2], lambda m: ghost[1, m])
            if s + 1 < SECTIONS:
                send_face(s + 1, 1 - face)

    for s in range(SECTIONS):
        for side in (0, 1):
            halo_copy(s, side).wait_send()
        for face in (0, 1):
            @pl.when(has[1 - face])
            def _():
                for d in order:
                    face_copy(s, face, d).wait_send()

            @pl.when(has[face])
            def _():
                for d in order:
                    forward_copy(s, face, d).wait_send()


def local(flow_state, velocity, offsets, passage_shift, donor_step, donor_weight):
    rows, count = lax.axis_size("row"), lax.axis_size("circ")
    comps, planes, radial, cells = flow_state.shape
    assert cells == LANES and 2 * planes * (radial // GROUP) == LANES
    vmem = pl.BlockSpec(memory_space=pltpu.VMEM)
    smem = pl.BlockSpec(memory_space=pltpu.SMEM)
    half = count // 2
    return pl.pallas_call(
        functools.partial(kernel, rows, count),
        out_shape=jax.ShapeDtypeStruct(flow_state.shape, flow_state.dtype),
        in_specs=[vmem, vmem, smem, smem, vmem, vmem],
        out_specs=vmem,
        scratch_shapes=[
            pltpu.VMEM(flow_state.shape, jnp.float32),
            pltpu.VMEM(flow_state.shape, jnp.float32),
            pltpu.VMEM((SECTIONS, comps, GROUP, cells), jnp.float32),
            pltpu.VMEM((SECTIONS, 2, comps, GROUP, cells), jnp.float32),
            pltpu.VMEM((comps, GROUP, cells), jnp.float32),
            pltpu.VMEM((2, 3 * cells, 2 * cells), jnp.bfloat16),
            pltpu.VMEM((2, comps, radial, cells), jnp.float32),
            pltpu.SemaphoreType.DMA((SECTIONS, 2, half)),
            pltpu.SemaphoreType.DMA((SECTIONS, 2, half)),
            pltpu.SemaphoreType.DMA((SECTIONS, 2, count)),
            pltpu.SemaphoreType.DMA((SECTIONS, 2)),
            pltpu.SemaphoreType.DMA((SECTIONS, 2)),
        ]
        + [pltpu.VMEM((count, comps, radial, cells), jnp.float32)] * (2 * SECTIONS),
        compiler_params=pltpu.CompilerParams(
            collective_id=0, has_side_effects=True, vmem_limit_bytes=44 * 1024 * 1024
        ),
    )(flow_state, velocity, offsets, passage_shift, donor_step, donor_weight)


def solution(mesh):
    placed = (
        P(None, "row", None, "circ"),
        P(None, "row", None, "circ"),
        P(),
        P(),
        P("row", None, "circ"),
        P("row", None, "circ"),
    )
    return jax.shard_map(
        local, mesh=mesh, in_specs=placed, out_specs=P(None, "row", None, "circ"), check_vma=False
    )
```

```python
import functools

import jax
import jax.numpy as jnp
from jax import lax
from jax.experimental import pallas as pl
from jax.experimental.pallas import tpu as pltpu
from jax.sharding import PartitionSpec as P

SMAG_COEF = 0.1
TIME_STEP = 0.25
SECTIONS = 3
LANES = 128
GROUP = 8


def kernel(
    row_count, count,
    q_in, u_in, off_in, shift_in, step_in, weight_in, out_ref,
    q_ref, u_ref, off_ref, shift_ref, step_ref, weight_ref,
    v1, v2, v3, pack, halo, comb, sel, ghost, share, shared, their_step, their_weight,
    send_sem, recv_sem, share_send, share_recv, halo_send, halo_recv, load_sem, store_sem, donor_send, donor_recv,
    *slots
):
    comps, planes, radial, cells = q_ref.shape
    groups = radial // GROUP
    half = count // 2
    loop_cells = count * cells
    row = lax.axis_index("row")
    col = lax.axis_index("circ")
    odd = lax.rem(col, 2)
    partner = col + 1 - 2 * odd
    right = lax.rem(col + 1, count)
    left = lax.rem(col + count - 1, count)
    has = (row > 0, row < row_count - 1)
    other_row = (row - 1, row + 1)
    fields = (q_ref, v1, v2, v3)
    order = sorted(range(half), key=lambda d: (min(d, half - d), d))

    lane = lax.broadcasted_iota(jnp.int32, (radial, cells), 1)
    line = lax.broadcasted_iota(jnp.int32, (radial, cells), 0)
    lane8 = lax.broadcasted_iota(jnp.int32, (GROUP, cells), 1)
    is_first, is_last = lane == 0, lane == cells - 1
    is_inner, is_outer = line == 0, line == radial - 1

    def away(d):
        return lax.rem(col + 2 * d, count)

    def back(d):
        return lax.rem(col + count - 2 * d, count)

    def face_copy(s, face, d):
        plane = planes - 1 if face == 0 else 0
        return pltpu.make_async_remote_copy(
            src_ref=(q_in if s == 0 else fields[s]).at[:, plane],
            dst_ref=slots[2 * s + face].at[col // 2],
            send_sem=send_sem.at[s, face, d],
            recv_sem=recv_sem.at[s, face, col // 2],
            device_id={"row": other_row[1 - face], "circ": away(d)},
            device_id_type=pl.DeviceIdType.MESH,
        )

    def share_copy(s, face):
        return pltpu.make_async_remote_copy(
            src_ref=share.at[s, face],
            dst_ref=shared.at[s, face],
            send_sem=share_send.at[s, face],
            recv_sem=share_recv.at[s, face],
            device_id={"row": row, "circ": partner},
            device_id_type=pl.DeviceIdType.MESH,
        )

    def arrival(s, face, slot):
        return pltpu.make_async_remote_copy(
            src_ref=slots[2 * s + face].at[slot],
            dst_ref=slots[2 * s + face].at[slot],
            send_sem=share_send.at[s, face],
            recv_sem=recv_sem.at[s, face, slot],
            device_id={"row": row, "circ": partner},
            device_id_type=pl.DeviceIdType.MESH,
        )

    def donor_copy(k):
        return pltpu.make_async_remote_copy(
            src_ref=(step_in, weight_in)[k],
            dst_ref=(their_step, their_weight)[k],
            send_sem=donor_send.at[k],
            recv_sem=donor_recv.at[k],
            device_id={"row": row, "circ": partner},
            device_id_type=pl.DeviceIdType.MESH,
        )

    def halo_copy(s, side):
        return pltpu.make_async_remote_copy(
            src_ref=pack.at[s],
            dst_ref=halo.at[s, side],
            send_sem=halo_send.at[s, side],
            recv_sem=halo_recv.at[s, side],
            device_id={"row": row, "circ": right if side == 0 else left},
            device_id_type=pl.DeviceIdType.MESH,
        )

    def send_face(s, face):
        @pl.when(has[1 - face])
        def _():
            for d in order:
                face_copy(s, face, d).start()

    def send_halo(s):
        halo_copy(s, 0).start()
        halo_copy(s, 1).start()

    def put_ends(s, m, a, value):
        packed = pack[s, m]
        for g in range(groups):
            spot = 2 * (a * groups + g)
            here = jnp.bitwise_and(lane8 + 1 - spot, cells - 1) < 2
            moved = pltpu.roll(value[g * GROUP:(g + 1) * GROUP], spot, 1)
            packed = jnp.where(here, moved, packed)
        pack[s, m] = packed

    def donor_base(s, face):
        source = jnp.clip(other_row[face], 0, row_count - 1)
        at = jnp.clip(row - 1 + face, 0, row_count - 2)
        offset = off_ref[s, at]
        offset = offset if face == 0 else lax.rem(loop_cells - offset, loop_cells)
        hop = lax.rem(shift_ref[source] - shift_ref[row] + offset // cells + count, count)
        first = col - odd + hop + lax.rem(odd + hop, 2)
        return hop, lax.rem(offset, cells), first

    def build_select(s):
        spots = lax.broadcasted_iota(jnp.int32, (cells, cells), 0)
        within = lax.broadcasted_iota(jnp.int32, (1, cells), 1)
        for face in (0, 1):
            hop, start, first = donor_base(s, face)
            for which, (who, steps) in enumerate(((col, step_ref), (partner, their_step))):
                donor = within + start + steps[0, face:face + 1, :]
                for k in (0, 1):
                    place = lax.rem(first + 2 * k - who - hop + 2 * count, count) * cells
                    for nxt in (0, 1):
                        hot = jnp.where(spots == donor + (nxt - place), 1.0, 0.0).astype(jnp.bfloat16)
                        at = (2 * which + nxt) * cells
                        sel[face, k * cells:(k + 1) * cells, at:at + cells] = hot

    def make_share(s, face):
        @pl.when(has[face])
        def _():
            for d in order:
                arrival(s, face, back(d) // 2).wait_recv()
            _, _, first = donor_base(s, face)
            base = first // 2
            blocks = [
                slots[2 * s + face][lax.rem(base + k, half)].reshape(comps * radial, cells) for k in (0, 1)
            ]
            block = jnp.concatenate(blocks, axis=1)
            high = block.astype(jnp.bfloat16)
            low = (block - high.astype(jnp.float32)).astype(jnp.bfloat16)

            def picked(which, weights):
                part = sel[face, :, 2 * which * cells:2 * (which + 1) * cells]
                total = jnp.dot(high, part, preferred_element_type=jnp.float32) + jnp.dot(
                    low, part, preferred_element_type=jnp.float32
                )
                weight = weights[0, face:face + 1, :]
                value = weight * total[:, :cells] + (1.0 - weight) * total[:, cells:]
                return value.reshape(comps, radial, cells)

            share[s, face] = picked(1, their_weight)
            share_copy(s, face).start()
            ghost[face] = picked(0, weight_ref)

    def make_ghost(s, face):
        @pl.when(has[face])
        def _():
            share_copy(s, face).wait_recv()
            ghost[face] = ghost[face] + shared[s, face]

        @pl.when(jnp.logical_not(has[face]))
        def _():
            ghost[face] = fields[s][:, 0 if face == 0 else planes - 1]

    def update(s, a, lower, upper):
        src, dst = fields[s], fields[s + 1]
        u_ax, u_rad, u_circ = 0.5 * u_ref[0, a], 0.5 * u_ref[1, a], 0.5 * u_ref[2, a]

        def terms(m):
            v, lo, hi = src[m, a], lower(m), upper(m)
            inner = jnp.where(is_inner, v, pltpu.roll(v, 1, 0))
            outer = jnp.where(is_outer, v, pltpu.roll(v, radial - 1, 0))
            edge = comb[m]
            ends = jnp.concatenate(
                [
                    pltpu.roll(edge, jnp.bitwise_and(2 * cells - 2 * (a * groups + g), cells - 1), 1)
                    for g in range(groups)
                ],
                axis=0,
            )
            before = pltpu.roll(jnp.where(is_last, ends, v), 1, 1)
            after = pltpu.roll(jnp.where(is_first, ends, v), cells - 1, 1)
            d_ax, d_rad, d_circ = hi - lo, outer - inner, after - before
            lap = ((hi + lo) + (outer + inner)) + ((after + before) - 6.0 * v)
            adv = u_ax * d_ax + u_rad * d_rad + u_circ * d_circ
            return v, d_ax, d_rad, d_circ, lap, adv

        def finish(m, v, lap, adv, nu):
            rate = nu * lap - adv
            if s == 0:
                new = v + TIME_STEP * rate
            elif s == 1:
                new = 0.75 * q_ref[m, a] + 0.25 * (v + TIME_STEP * rate)
            else:
                new = (1.0 / 3.0) * q_ref[m, a] + (2.0 / 3.0) * (v + TIME_STEP * rate)
            dst[m, a] = new
            if s + 1 < SECTIONS:
                put_ends(s + 1, m, a, new)

        strain = jnp.zeros((radial, cells), jnp.float32)
        held = []
        for m in (1, 2, 3):
            v, d_ax, d_rad, d_circ, lap, adv = terms(m)
            strain = strain + (d_ax * d_ax + d_rad * d_rad + d_circ * d_circ)
            held.append((m, v, lap, adv))
        nu = SMAG_COEF * jnp.sqrt(0.25 * strain + 1.0)
        for m, v, lap, adv in held:
            finish(m, v, lap, adv, nu)
        for m in (0, *range(4, comps)):
            v, _, _, _, lap, adv = terms(m)
            finish(m, v, lap, adv, nu)

    def inside(s, first, last):
        src = fields[s]

        def body(a, carry):
            update(s, a, lambda m: src[m, a - 1], lambda m: src[m, a + 1])
            return carry

        lax.fori_loop(first, last, body, 0)

    barrier = pltpu.get_barrier_semaphore()
    for side in (left, right):
        pl.semaphore_signal(
            barrier, inc=1, device_id={"row": row, "circ": side}, device_id_type=pl.DeviceIdType.MESH
        )
    for face in (0, 1):
        @pl.when(has[face])
        def _():
            for d in range(half):
                pl.semaphore_signal(
                    barrier, inc=1, device_id={"row": other_row[face], "circ": away(d)},
                    device_id_type=pl.DeviceIdType.MESH,
                )

    loads = [
        pltpu.make_async_copy(source, target, load_sem.at[k])
        for k, (source, target) in enumerate((
            (q_in, q_ref), (u_in, u_ref), (off_in, off_ref), (shift_in, shift_ref),
            (step_in, step_ref), (weight_in, weight_ref),
        ))
    ]
    for load in loads:
        load.start()
    pack[...] = jnp.zeros_like(pack)
    pl.semaphore_wait(barrier, 2 + half * (has[0].astype(jnp.int32) + has[1].astype(jnp.int32)))
    send_face(0, 0)
    send_face(0, 1)
    for k in (0, 1):
        donor_copy(k).start()
    for load in loads:
        load.wait()

    def first_ends(a, carry):
        for m in range(comps):
            put_ends(0, m, a, q_ref[m, a])
        return carry

    lax.fori_loop(0, planes, first_ends, 0)
    for k in (0, 1):
        donor_copy(k).wait_recv()

    middle = max(1, planes * 5 // 8)
    stores = [
        pltpu.make_async_copy(v3.at[:, a:b], out_ref.at[:, a:b], store_sem.at[k])
        for k, (a, b) in enumerate(((1, planes - 1), (0, 1), (planes - 1, planes)))
    ]
    for s in range(SECTIONS):
        src = fields[s]
        send_halo(s)
        build_select(s)
        for side in (0, 1):
            halo_copy(s, side).wait_recv()
        for m in range(comps):
            comb[m] = jnp.where(jnp.bitwise_and(lane8, 1) == 0, halo[s, 1, m], halo[s, 0, m])
        inside(s, 1, middle)
        for face in (0, 1):
            make_share(s, face)
        inside(s, middle, planes - 1)
        if s + 1 == SECTIONS:
            stores[0].start()
        for face in (0, 1):
            make_ghost(s, face)
            if face == 0:
                update(s, 0, lambda m: ghost[0, m], lambda m: src[m, 1])
            else:
                update(s, planes - 1, lambda m: src[m, planes - 2], lambda m: ghost[1, m])
            if s + 1 < SECTIONS:
                send_face(s + 1, 1 - face)
            else:
                stores[1 + face].start()

    for store in stores:
        store.wait()
    for k in (0, 1):
        donor_copy(k).wait_send()
    for s in range(SECTIONS):
        for side in (0, 1):
            halo_copy(s, side).wait_send()
        for face in (0, 1):
            @pl.when(has[1 - face])
            def _():
                for d in order:
                    face_copy(s, face, d).wait_send()

            @pl.when(has[face])
            def _():
                share_copy(s, face).wait_send()


def local(flow_state, velocity, offsets, passage_shift, donor_step, donor_weight):
    rows, count = lax.axis_size("row"), lax.axis_size("circ")
    comps, planes, radial, cells = flow_state.shape
    assert cells == LANES and 2 * planes * (radial // GROUP) == LANES
    whole = pl.BlockSpec(memory_space=pl.ANY)
    half = count // 2
    face = (comps, radial, cells)
    return pl.pallas_call(
        functools.partial(kernel, rows, count),
        out_shape=jax.ShapeDtypeStruct(flow_state.shape, flow_state.dtype),
        in_specs=[whole] * 6,
        out_specs=whole,
        scratch_shapes=[
            pltpu.VMEM(flow_state.shape, jnp.float32),
            pltpu.VMEM(velocity.shape, jnp.float32),
            pltpu.SMEM(offsets.shape, jnp.int32),
            pltpu.SMEM(passage_shift.shape, jnp.int32),
            pltpu.VMEM(donor_step.shape, jnp.int32),
            pltpu.VMEM(donor_weight.shape, jnp.float32),
            pltpu.VMEM(flow_state.shape, jnp.float32),
            pltpu.VMEM(flow_state.shape, jnp.float32),
            pltpu.VMEM(flow_state.shape, jnp.float32),
            pltpu.VMEM((SECTIONS, comps, GROUP, cells), jnp.float32),
            pltpu.VMEM((SECTIONS, 2, comps, GROUP, cells), jnp.float32),
            pltpu.VMEM((comps, GROUP, cells), jnp.float32),
            pltpu.VMEM((2, 2 * cells, 4 * cells), jnp.bfloat16),
            pltpu.VMEM((2, *face), jnp.float32),
            pltpu.VMEM((SECTIONS, 2, *face), jnp.float32),
            pltpu.VMEM((SECTIONS, 2, *face), jnp.float32),
            pltpu.VMEM(donor_step.shape, jnp.int32),
            pltpu.VMEM(donor_weight.shape, jnp.float32),
            pltpu.SemaphoreType.DMA((SECTIONS, 2, half)),
            pltpu.SemaphoreType.DMA((SECTIONS, 2, half)),
            pltpu.SemaphoreType.DMA((SECTIONS, 2)),
            pltpu.SemaphoreType.DMA((SECTIONS, 2)),
            pltpu.SemaphoreType.DMA((SECTIONS, 2)),
            pltpu.SemaphoreType.DMA((SECTIONS, 2)),
            pltpu.SemaphoreType.DMA((6,)),
            pltpu.SemaphoreType.DMA((3,)),
            pltpu.SemaphoreType.DMA((2,)),
            pltpu.SemaphoreType.DMA((2,)),
        ]
        + [pltpu.VMEM((half, *face), jnp.float32)] * (2 * SECTIONS),
        compiler_params=pltpu.CompilerParams(
            collective_id=0, has_side_effects=True, vmem_limit_bytes=44 * 1024 * 1024
        ),
    )(flow_state, velocity, offsets, passage_shift, donor_step, donor_weight)


def solution(mesh):
    placed = (
        P(None, "row", None, "circ"),
        P(None, "row", None, "circ"),
        P(),
        P(),
        P("row", None, "circ"),
        P("row", None, "circ"),
    )
    return jax.shard_map(
        local, mesh=mesh, in_specs=placed, out_specs=P(None, "row", None, "circ"), check_vma=False
    )
```

```python
import functools

import jax
import jax.numpy as jnp
from jax import lax
from jax.experimental import pallas as pl
from jax.experimental.pallas import tpu as pltpu
from jax.sharding import PartitionSpec as P

SMAG_COEF = 0.1
TIME_STEP = 0.25
SECTIONS = 3
LANES = 128
GROUP = 8


def kernel(
    row_count, count,
    q_in, u_in, off_in, shift_in, step_in, weight_in, out_ref,
    q_ref, u_ref, off_ref, shift_ref, step_ref, weight_ref,
    v1, v2, v3, pack, halo, comb, sel, ghost, share, shared, their_step, their_weight,
    send_sem, relay_send, recv_sem, share_send, share_recv, halo_send, halo_recv, load_sem, store_sem, donor_send, donor_recv,
    *slots
):
    comps, planes, radial, cells = q_ref.shape
    groups = radial // GROUP
    half = count // 2
    loop_cells = count * cells
    row = lax.axis_index("row")
    col = lax.axis_index("circ")
    odd = lax.rem(col, 2)
    partner = col + 1 - 2 * odd
    right = lax.rem(col + 1, count)
    left = lax.rem(col + count - 1, count)
    has = (row > 0, row < row_count - 1)
    other_row = (row - 1, row + 1)
    fields = (q_ref, v1, v2, v3)
    spot_in_line = col // 2
    not_low, not_high = spot_in_line > 0, spot_in_line < half - 1

    lane = lax.broadcasted_iota(jnp.int32, (radial, cells), 1)
    line = lax.broadcasted_iota(jnp.int32, (radial, cells), 0)
    lane8 = lax.broadcasted_iota(jnp.int32, (GROUP, cells), 1)
    is_first, is_last = lane == 0, lane == cells - 1
    is_inner, is_outer = line == 0, line == radial - 1

    def reaches(step):
        return {0: row >= 0, 1: not_high, -1: not_low}[step]

    def face_copy(s, face, step):
        plane = planes - 1 if face == 0 else 0
        return pltpu.make_async_remote_copy(
            src_ref=(q_in if s == 0 else fields[s]).at[:, plane],
            dst_ref=slots[2 * s + face].at[col // 2],
            send_sem=send_sem.at[s, face, step + 1],
            recv_sem=recv_sem.at[s, face, col // 2],
            device_id={"row": other_row[1 - face], "circ": col + 2 * step},
            device_id_type=pl.DeviceIdType.MESH,
        )

    def relay_copy(s, face, slot, step):
        return pltpu.make_async_remote_copy(
            src_ref=slots[2 * s + face].at[slot],
            dst_ref=slots[2 * s + face].at[slot],
            send_sem=relay_send.at[s, face, slot],
            recv_sem=recv_sem.at[s, face, slot],
            device_id={"row": row, "circ": col + 2 * step},
            device_id_type=pl.DeviceIdType.MESH,
        )

    def share_copy(s, face):
        return pltpu.make_async_remote_copy(
            src_ref=share.at[s, face],
            dst_ref=shared.at[s, face],
            send_sem=share_send.at[s, face],
            recv_sem=share_recv.at[s, face],
            device_id={"row": row, "circ": partner},
            device_id_type=pl.DeviceIdType.MESH,
        )

    def arrival(s, face, slot):
        return pltpu.make_async_remote_copy(
            src_ref=slots[2 * s + face].at[slot],
            dst_ref=slots[2 * s + face].at[slot],
            send_sem=share_send.at[s, face],
            recv_sem=recv_sem.at[s, face, slot],
            device_id={"row": row, "circ": partner},
            device_id_type=pl.DeviceIdType.MESH,
        )

    def donor_copy(k):
        return pltpu.make_async_remote_copy(
            src_ref=(step_in, weight_in)[k],
            dst_ref=(their_step, their_weight)[k],
            send_sem=donor_send.at[k],
            recv_sem=donor_recv.at[k],
            device_id={"row": row, "circ": partner},
            device_id_type=pl.DeviceIdType.MESH,
        )

    def halo_copy(s, side):
        return pltpu.make_async_remote_copy(
            src_ref=pack.at[s],
            dst_ref=halo.at[s, side],
            send_sem=halo_send.at[s, side],
            recv_sem=halo_recv.at[s, side],
            device_id={"row": row, "circ": right if side == 0 else left},
            device_id_type=pl.DeviceIdType.MESH,
        )

    def send_face(s, face):
        @pl.when(has[1 - face])
        def _():
            for step in (1, -1, 0):
                @pl.when(reaches(step))
                def _():
                    face_copy(s, face, step).start()

    def relay(s, distance):
        for face in (0, 1):
            for step in (1, -1):
                slot = spot_in_line - step * distance
                @pl.when(has[face] & (slot >= 0) & (slot < half))
                def _():
                    arrival(s, face, slot).wait_recv()

                    @pl.when(reaches(step))
                    def _():
                        relay_copy(s, face, slot, step).start()

    def send_halo(s):
        halo_copy(s, 0).start()
        halo_copy(s, 1).start()

    def put_ends(s, m, a, value):
        packed = pack[s, m]
        for g in range(groups):
            spot = 2 * (a * groups + g)
            here = jnp.bitwise_and(lane8 + 1 - spot, cells - 1) < 2
            moved = pltpu.roll(value[g * GROUP:(g + 1) * GROUP], spot, 1)
            packed = jnp.where(here, moved, packed)
        pack[s, m] = packed

    def donor_base(s, face):
        source = jnp.clip(other_row[face], 0, row_count - 1)
        at = jnp.clip(row - 1 + face, 0, row_count - 2)
        offset = off_ref[s, at]
        offset = offset if face == 0 else lax.rem(loop_cells - offset, loop_cells)
        hop = lax.rem(shift_ref[source] - shift_ref[row] + offset // cells + count, count)
        first = col - odd + hop + lax.rem(odd + hop, 2)
        return hop, lax.rem(offset, cells), first

    def build_select(s):
        spots = lax.broadcasted_iota(jnp.int32, (cells, cells), 0)
        within = lax.broadcasted_iota(jnp.int32, (1, cells), 1)
        for face in (0, 1):
            hop, start, first = donor_base(s, face)
            for which, (who, steps) in enumerate(((col, step_ref), (partner, their_step))):
                donor = within + start + steps[0, face:face + 1, :]
                for k in (0, 1):
                    place = lax.rem(first + 2 * k - who - hop + 2 * count, count) * cells
                    for nxt in (0, 1):
                        hot = jnp.where(spots == donor + (nxt - place), 1.0, 0.0).astype(jnp.bfloat16)
                        at = (2 * which + nxt) * cells
                        sel[face, k * cells:(k + 1) * cells, at:at + cells] = hot

    def make_share(s, face):
        @pl.when(has[face])
        def _():
            arrival(s, face, spot_in_line).wait_recv()
            _, _, first = donor_base(s, face)
            base = first // 2
            blocks = [
                slots[2 * s + face][lax.rem(base + k, half)].reshape(comps * radial, cells) for k in (0, 1)
            ]
            block = jnp.concatenate(blocks, axis=1)
            high = block.astype(jnp.bfloat16)
            low = (block - high.astype(jnp.float32)).astype(jnp.bfloat16)

            def picked(which, weights):
                part = sel[face, :, 2 * which * cells:2 * (which + 1) * cells]
                total = jnp.dot(high, part, preferred_element_type=jnp.float32) + jnp.dot(
                    low, part, preferred_element_type=jnp.float32
                )
                weight = weights[0, face:face + 1, :]
                value = weight * total[:, :cells] + (1.0 - weight) * total[:, cells:]
                return value.reshape(comps, radial, cells)

            share[s, face] = picked(1, their_weight)
            share_copy(s, face).start()
            ghost[face] = picked(0, weight_ref)

    def make_ghost(s, face):
        @pl.when(has[face])
        def _():
            share_copy(s, face).wait_recv()
            ghost[face] = ghost[face] + shared[s, face]

        @pl.when(jnp.logical_not(has[face]))
        def _():
            ghost[face] = fields[s][:, 0 if face == 0 else planes - 1]

    def update(s, a, lower, upper):
        src, dst = fields[s], fields[s + 1]
        u_ax, u_rad, u_circ = 0.5 * u_ref[0, a], 0.5 * u_ref[1, a], 0.5 * u_ref[2, a]

        def terms(m):
            v, lo, hi = src[m, a], lower(m), upper(m)
            inner = jnp.where(is_inner, v, pltpu.roll(v, 1, 0))
            outer = jnp.where(is_outer, v, pltpu.roll(v, radial - 1, 0))
            edge = comb[m]
            ends = jnp.concatenate(
                [
                    pltpu.roll(edge, jnp.bitwise_and(2 * cells - 2 * (a * groups + g), cells - 1), 1)
                    for g in range(groups)
                ],
                axis=0,
            )
            before = pltpu.roll(jnp.where(is_last, ends, v), 1, 1)
            after = pltpu.roll(jnp.where(is_first, ends, v), cells - 1, 1)
            d_ax, d_rad, d_circ = hi - lo, outer - inner, after - before
            lap = ((hi + lo) + (outer + inner)) + ((after + before) - 6.0 * v)
            adv = u_ax * d_ax + u_rad * d_rad + u_circ * d_circ
            return v, d_ax, d_rad, d_circ, lap, adv

        def finish(m, v, lap, adv, nu):
            rate = nu * lap - adv
            if s == 0:
                new = v + TIME_STEP * rate
            elif s == 1:
                new = 0.75 * q_ref[m, a] + 0.25 * (v + TIME_STEP * rate)
            else:
                new = (1.0 / 3.0) * q_ref[m, a] + (2.0 / 3.0) * (v + TIME_STEP * rate)
            dst[m, a] = new
            if s + 1 < SECTIONS:
                put_ends(s + 1, m, a, new)

        strain = jnp.zeros((radial, cells), jnp.float32)
        held = []
        for m in (1, 2, 3):
            v, d_ax, d_rad, d_circ, lap, adv = terms(m)
            strain = strain + (d_ax * d_ax + d_rad * d_rad + d_circ * d_circ)
            held.append((m, v, lap, adv))
        nu = SMAG_COEF * jnp.sqrt(0.25 * strain + 1.0)
        for m, v, lap, adv in held:
            finish(m, v, lap, adv, nu)
        for m in (0, *range(4, comps)):
            v, _, _, _, lap, adv = terms(m)
            finish(m, v, lap, adv, nu)

    def inside(s, first, last):
        src = fields[s]

        def body(a, carry):
            update(s, a, lambda m: src[m, a - 1], lambda m: src[m, a + 1])
            return carry

        lax.fori_loop(first, last, body, 0)

    barrier = pltpu.get_barrier_semaphore()
    for side in (left, right):
        pl.semaphore_signal(
            barrier, inc=1, device_id={"row": row, "circ": side}, device_id_type=pl.DeviceIdType.MESH
        )
    for face in (0, 1):
        @pl.when(has[face])
        def _():
            for step in (0, 1, -1):
                @pl.when(reaches(step))
                def _():
                    pl.semaphore_signal(
                        barrier, inc=1, device_id={"row": other_row[face], "circ": col + 2 * step},
                        device_id_type=pl.DeviceIdType.MESH,
                    )
    for step in (1, -1):
        @pl.when(reaches(step))
        def _():
            pl.semaphore_signal(
                barrier, inc=1, device_id={"row": row, "circ": col + 2 * step},
                device_id_type=pl.DeviceIdType.MESH,
            )

    loads = [
        pltpu.make_async_copy(source, target, load_sem.at[k])
        for k, (source, target) in enumerate((
            (q_in, q_ref), (u_in, u_ref), (off_in, off_ref), (shift_in, shift_ref),
            (step_in, step_ref), (weight_in, weight_ref),
        ))
    ]
    for load in loads:
        load.start()
    pack[...] = jnp.zeros_like(pack)
    line_sides = not_low.astype(jnp.int32) + not_high.astype(jnp.int32)
    pl.semaphore_wait(
        barrier, 2 + line_sides + (1 + line_sides) * (has[0].astype(jnp.int32) + has[1].astype(jnp.int32))
    )
    send_face(0, 0)
    send_face(0, 1)
    for k in (0, 1):
        donor_copy(k).start()
    for load in loads:
        load.wait()

    def first_ends(a, carry):
        for m in range(comps):
            put_ends(0, m, a, q_ref[m, a])
        return carry

    lax.fori_loop(0, planes, first_ends, 0)
    for k in (0, 1):
        donor_copy(k).wait_recv()

    middle = planes * 5 // 8
    cuts = [1 + (middle - 1) * i // (half - 1) for i in range(half)]
    stores = [
        pltpu.make_async_copy(v3.at[:, a:b], out_ref.at[:, a:b], store_sem.at[k])
        for k, (a, b) in enumerate(((1, planes - 1), (0, 1), (planes - 1, planes)))
    ]
    for s in range(SECTIONS):
        src = fields[s]
        send_halo(s)
        build_select(s)
        for side in (0, 1):
            halo_copy(s, side).wait_recv()
        for m in range(comps):
            comb[m] = jnp.where(jnp.bitwise_and(lane8, 1) == 0, halo[s, 1, m], halo[s, 0, m])
        for i in range(half - 1):
            if cuts[i] < cuts[i + 1]:
                inside(s, cuts[i], cuts[i + 1])
            relay(s, i + 1)
        for face in (0, 1):
            make_share(s, face)
        inside(s, middle, planes - 1)
        if s + 1 == SECTIONS:
            stores[0].start()
        for face in (0, 1):
            make_ghost(s, face)
            if face == 0:
                update(s, 0, lambda m: ghost[0, m], lambda m: src[m, 1])
            else:
                update(s, planes - 1, lambda m: src[m, planes - 2], lambda m: ghost[1, m])
            if s + 1 < SECTIONS:
                send_face(s + 1, 1 - face)
            else:
                stores[1 + face].start()

    for store in stores:
        store.wait()
    for k in (0, 1):
        donor_copy(k).wait_send()
    for s in range(SECTIONS):
        for side in (0, 1):
            halo_copy(s, side).wait_send()
        for face in (0, 1):
            @pl.when(has[1 - face])
            def _():
                for step in (1, -1, 0):
                    @pl.when(reaches(step))
                    def _():
                        face_copy(s, face, step).wait_send()

            @pl.when(has[face])
            def _():
                share_copy(s, face).wait_send()
                for slot in range(half):
                    @pl.when(((spot_in_line > slot) & not_high) | ((spot_in_line < slot) & not_low))
                    def _():
                        relay_copy(s, face, slot, 1).wait_send()


def local(flow_state, velocity, offsets, passage_shift, donor_step, donor_weight):
    rows, count = lax.axis_size("row"), lax.axis_size("circ")
    comps, planes, radial, cells = flow_state.shape
    assert cells == LANES and 2 * planes * (radial // GROUP) == LANES
    whole = pl.BlockSpec(memory_space=pl.ANY)
    half = count // 2
    face = (comps, radial, cells)
    return pl.pallas_call(
        functools.partial(kernel, rows, count),
        out_shape=jax.ShapeDtypeStruct(flow_state.shape, flow_state.dtype),
        in_specs=[whole] * 6,
        out_specs=whole,
        scratch_shapes=[
            pltpu.VMEM(flow_state.shape, jnp.float32),
            pltpu.VMEM(velocity.shape, jnp.float32),
            pltpu.SMEM(offsets.shape, jnp.int32),
            pltpu.SMEM(passage_shift.shape, jnp.int32),
            pltpu.VMEM(donor_step.shape, jnp.int32),
            pltpu.VMEM(donor_weight.shape, jnp.float32),
            pltpu.VMEM(flow_state.shape, jnp.float32),
            pltpu.VMEM(flow_state.shape, jnp.float32),
            pltpu.VMEM(flow_state.shape, jnp.float32),
            pltpu.VMEM((SECTIONS, comps, GROUP, cells), jnp.float32),
            pltpu.VMEM((SECTIONS, 2, comps, GROUP, cells), jnp.float32),
            pltpu.VMEM((comps, GROUP, cells), jnp.float32),
            pltpu.VMEM((2, 2 * cells, 4 * cells), jnp.bfloat16),
            pltpu.VMEM((2, *face), jnp.float32),
            pltpu.VMEM((SECTIONS, 2, *face), jnp.float32),
            pltpu.VMEM((SECTIONS, 2, *face), jnp.float32),
            pltpu.VMEM(donor_step.shape, jnp.int32),
            pltpu.VMEM(donor_weight.shape, jnp.float32),
            pltpu.SemaphoreType.DMA((SECTIONS, 2, 3)),
            pltpu.SemaphoreType.DMA((SECTIONS, 2, half)),
            pltpu.SemaphoreType.DMA((SECTIONS, 2, half)),
            pltpu.SemaphoreType.DMA((SECTIONS, 2)),
            pltpu.SemaphoreType.DMA((SECTIONS, 2)),
            pltpu.SemaphoreType.DMA((SECTIONS, 2)),
            pltpu.SemaphoreType.DMA((SECTIONS, 2)),
            pltpu.SemaphoreType.DMA((6,)),
            pltpu.SemaphoreType.DMA((3,)),
            pltpu.SemaphoreType.DMA((2,)),
            pltpu.SemaphoreType.DMA((2,)),
        ]
        + [pltpu.VMEM((half, *face), jnp.float32)] * (2 * SECTIONS),
        compiler_params=pltpu.CompilerParams(
            collective_id=0, has_side_effects=True, vmem_limit_bytes=63 * 1024 * 1024
        ),
    )(flow_state, velocity, offsets, passage_shift, donor_step, donor_weight)


def solution(mesh):
    placed = (
        P(None, "row", None, "circ"),
        P(None, "row", None, "circ"),
        P(),
        P(),
        P("row", None, "circ"),
        P("row", None, "circ"),
    )
    return jax.shard_map(
        local, mesh=mesh, in_specs=placed, out_specs=P(None, "row", None, "circ"), check_vma=False
    )
```

```python
import functools

import jax
import jax.numpy as jnp
from jax import lax
from jax.experimental import pallas as pl
from jax.experimental.pallas import tpu as pltpu
from jax.sharding import PartitionSpec as P

SMAG_COEF = 0.1
TIME_STEP = 0.25
SECTIONS = 3
LANES = 128
GROUP = 8


def kernel(
    row_count, count,
    q_in, u_in, off_in, shift_in, step_in, weight_in, out_ref,
    q_ref, u_ref, off_ref, shift_ref, step_ref, weight_ref,
    v1, v2, v3, pack, halo, comb, sel, ghost, share, shared, their_step, their_weight,
    send_sem, recv_sem, share_send, share_recv, halo_send, halo_recv, load_sem, store_sem, donor_send, donor_recv,
    *slots
):
    comps, planes, radial, cells = q_ref.shape
    groups = radial // GROUP
    half = count // 2
    loop_cells = count * cells
    row = lax.axis_index("row")
    col = lax.axis_index("circ")
    odd = lax.rem(col, 2)
    partner = col + 1 - 2 * odd
    right = lax.rem(col + 1, count)
    left = lax.rem(col + count - 1, count)
    has = (row > 0, row < row_count - 1)
    other_row = (row - 1, row + 1)
    fields = (q_ref, v1, v2, v3)
    order = sorted(range(half), key=lambda d: (min(d, half - d), d))

    lane = lax.broadcasted_iota(jnp.int32, (radial, cells), 1)
    line = lax.broadcasted_iota(jnp.int32, (radial, cells), 0)
    lane8 = lax.broadcasted_iota(jnp.int32, (GROUP, cells), 1)
    is_first, is_last = lane == 0, lane == cells - 1
    is_inner, is_outer = line == 0, line == radial - 1

    def away(d):
        return lax.rem(col + 2 * d, count)

    def back(d):
        return lax.rem(col + count - 2 * d, count)

    def face_copy(s, face, d):
        plane = planes - 1 if face == 0 else 0
        return pltpu.make_async_remote_copy(
            src_ref=(q_in if s == 0 else fields[s]).at[:, plane],
            dst_ref=slots[2 * s + face].at[col // 2],
            send_sem=send_sem.at[s, face, d],
            recv_sem=recv_sem.at[s, face, col // 2],
            device_id={"row": other_row[1 - face], "circ": away(d)},
            device_id_type=pl.DeviceIdType.MESH,
        )

    def share_copy(s, face):
        return pltpu.make_async_remote_copy(
            src_ref=share.at[s, face],
            dst_ref=shared.at[s, face],
            send_sem=share_send.at[s, face],
            recv_sem=share_recv.at[s, face],
            device_id={"row": row, "circ": partner},
            device_id_type=pl.DeviceIdType.MESH,
        )

    def arrival(s, face, slot):
        return pltpu.make_async_remote_copy(
            src_ref=slots[2 * s + face].at[slot],
            dst_ref=slots[2 * s + face].at[slot],
            send_sem=share_send.at[s, face],
            recv_sem=recv_sem.at[s, face, slot],
            device_id={"row": row, "circ": partner},
            device_id_type=pl.DeviceIdType.MESH,
        )

    def donor_copy(k):
        return pltpu.make_async_remote_copy(
            src_ref=(step_in, weight_in)[k],
            dst_ref=(their_step, their_weight)[k],
            send_sem=donor_send.at[k],
            recv_sem=donor_recv.at[k],
            device_id={"row": row, "circ": partner},
            device_id_type=pl.DeviceIdType.MESH,
        )

    def halo_copy(s, side):
        return pltpu.make_async_remote_copy(
            src_ref=pack.at[s],
            dst_ref=halo.at[s, side],
            send_sem=halo_send.at[s, side],
            recv_sem=halo_recv.at[s, side],
            device_id={"row": row, "circ": right if side == 0 else left},
            device_id_type=pl.DeviceIdType.MESH,
        )

    def send_face(s, face):
        @pl.when(has[1 - face])
        def _():
            for d in order:
                face_copy(s, face, d).start()

    def send_halo(s):
        halo_copy(s, 0).start()
        halo_copy(s, 1).start()

    def put_ends(s, m, a, value):
        packed = pack[s, m]
        for g in range(groups):
            spot = 2 * (a * groups + g)
            here = jnp.bitwise_and(lane8 + 1 - spot, cells - 1) < 2
            moved = pltpu.roll(value[g * GROUP:(g + 1) * GROUP], spot, 1)
            packed = jnp.where(here, moved, packed)
        pack[s, m] = packed

    def donor_base(s, face):
        source = jnp.clip(other_row[face], 0, row_count - 1)
        at = jnp.clip(row - 1 + face, 0, row_count - 2)
        offset = off_ref[s, at]
        offset = offset if face == 0 else lax.rem(loop_cells - offset, loop_cells)
        hop = lax.rem(shift_ref[source] - shift_ref[row] + offset // cells + count, count)
        first = col - odd + hop + lax.rem(odd + hop, 2)
        return hop, lax.rem(offset, cells), first

    def build_select(s):
        spots = lax.broadcasted_iota(jnp.int32, (cells, cells), 0)
        within = lax.broadcasted_iota(jnp.int32, (1, cells), 1)
        for face in (0, 1):
            hop, start, first = donor_base(s, face)
            for which, (who, steps) in enumerate(((col, step_ref), (partner, their_step))):
                donor = within + start + steps[0, face:face + 1, :]
                for k in (0, 1):
                    place = lax.rem(first + 2 * k - who - hop + 2 * count, count) * cells
                    for nxt in (0, 1):
                        hot = jnp.where(spots == donor + (nxt - place), 1.0, 0.0).astype(jnp.bfloat16)
                        at = (2 * which + nxt) * cells
                        sel[face, k * cells:(k + 1) * cells, at:at + cells] = hot

    def make_share(s, face):
        @pl.when(has[face])
        def _():
            for d in order:
                arrival(s, face, back(d) // 2).wait_recv()
            _, _, first = donor_base(s, face)
            base = first // 2
            blocks = [
                slots[2 * s + face][lax.rem(base + k, half)].reshape(comps * radial, cells) for k in (0, 1)
            ]
            block = jnp.concatenate(blocks, axis=1)
            high = block.astype(jnp.bfloat16)
            low = (block - high.astype(jnp.float32)).astype(jnp.bfloat16)

            def picked(which, weights):
                part = sel[face, :, 2 * which * cells:2 * (which + 1) * cells]
                total = jnp.dot(high, part, preferred_element_type=jnp.float32) + jnp.dot(
                    low, part, preferred_element_type=jnp.float32
                )
                weight = weights[0, face:face + 1, :]
                value = weight * total[:, :cells] + (1.0 - weight) * total[:, cells:]
                return value.reshape(comps, radial, cells)

            share[s, face] = picked(1, their_weight)
            share_copy(s, face).start()
            ghost[face] = picked(0, weight_ref)

    def make_ghost(s, face):
        @pl.when(has[face])
        def _():
            share_copy(s, face).wait_recv()
            ghost[face] = ghost[face] + shared[s, face]

        @pl.when(jnp.logical_not(has[face]))
        def _():
            ghost[face] = fields[s][:, 0 if face == 0 else planes - 1]

    def update(s, a, lower, upper):
        src, dst = fields[s], fields[s + 1]
        u_ax, u_rad, u_circ = 0.5 * u_ref[0, a], 0.5 * u_ref[1, a], 0.5 * u_ref[2, a]

        def terms(m):
            v, lo, hi = src[m, a], lower(m), upper(m)
            inner = jnp.where(is_inner, v, pltpu.roll(v, 1, 0))
            outer = jnp.where(is_outer, v, pltpu.roll(v, radial - 1, 0))
            edge = comb[m]
            ends = jnp.concatenate(
                [
                    pltpu.roll(edge, jnp.bitwise_and(2 * cells - 2 * (a * groups + g), cells - 1), 1)
                    for g in range(groups)
                ],
                axis=0,
            )
            before = pltpu.roll(jnp.where(is_last, ends, v), 1, 1)
            after = pltpu.roll(jnp.where(is_first, ends, v), cells - 1, 1)
            d_ax, d_rad, d_circ = hi - lo, outer - inner, after - before
            lap = ((hi + lo) + (outer + inner)) + ((after + before) - 6.0 * v)
            adv = u_ax * d_ax + u_rad * d_rad + u_circ * d_circ
            return v, d_ax, d_rad, d_circ, lap, adv

        def finish(m, v, lap, adv, nu):
            rate = nu * lap - adv
            if s == 0:
                new = v + TIME_STEP * rate
            elif s == 1:
                new = 0.75 * q_ref[m, a] + 0.25 * (v + TIME_STEP * rate)
            else:
                new = (1.0 / 3.0) * q_ref[m, a] + (2.0 / 3.0) * (v + TIME_STEP * rate)
            dst[m, a] = new
            if s + 1 < SECTIONS:
                put_ends(s + 1, m, a, new)

        strain = jnp.zeros((radial, cells), jnp.float32)
        held = []
        for m in (1, 2, 3):
            v, d_ax, d_rad, d_circ, lap, adv = terms(m)
            strain = strain + (d_ax * d_ax + d_rad * d_rad + d_circ * d_circ)
            held.append((m, v, lap, adv))
        nu = SMAG_COEF * jnp.sqrt(0.25 * strain + 1.0)
        for m, v, lap, adv in held:
            finish(m, v, lap, adv, nu)
        for m in (0, *range(4, comps)):
            v, _, _, _, lap, adv = terms(m)
            finish(m, v, lap, adv, nu)

    def inside(s, first, last):
        src = fields[s]

        def body(a, carry):
            update(s, a, lambda m: src[m, a - 1], lambda m: src[m, a + 1])
            return carry

        lax.fori_loop(first, last, body, 0)

    barrier = pltpu.get_barrier_semaphore()
    for side in (left, right):
        pl.semaphore_signal(
            barrier, inc=1, device_id={"row": row, "circ": side}, device_id_type=pl.DeviceIdType.MESH
        )
    for face in (0, 1):
        @pl.when(has[face])
        def _():
            for d in range(half):
                pl.semaphore_signal(
                    barrier, inc=1, device_id={"row": other_row[face], "circ": away(d)},
                    device_id_type=pl.DeviceIdType.MESH,
                )

    loads = [
        pltpu.make_async_copy(source, target, load_sem.at[k])
        for k, (source, target) in enumerate((
            (q_in, q_ref), (u_in, u_ref), (off_in, off_ref), (shift_in, shift_ref),
            (step_in, step_ref), (weight_in, weight_ref),
        ))
    ]
    for load in loads:
        load.start()
    pack[...] = jnp.zeros_like(pack)
    pl.semaphore_wait(barrier, 2 + half * (has[0].astype(jnp.int32) + has[1].astype(jnp.int32)))
    send_face(0, 0)
    send_face(0, 1)
    for k in (0, 1):
        donor_copy(k).start()
    for load in loads:
        load.wait()

    def first_ends(a, carry):
        for m in range(comps):
            put_ends(0, m, a, q_ref[m, a])
        return carry

    lax.fori_loop(0, planes, first_ends, 0)
    for k in (0, 1):
        donor_copy(k).wait_recv()

    middle = max(1, planes * 5 // 8)
    stores = [
        pltpu.make_async_copy(v3.at[:, a:b], out_ref.at[:, a:b], store_sem.at[k])
        for k, (a, b) in enumerate(((1, planes - 1), (0, 1), (planes - 1, planes)))
    ]
    for s in range(SECTIONS):
        src = fields[s]
        send_halo(s)
        build_select(s)
        for side in (0, 1):
            halo_copy(s, side).wait_recv()
        for m in range(comps):
            comb[m] = jnp.where(jnp.bitwise_and(lane8, 1) == 0, halo[s, 1, m], halo[s, 0, m])
        inside(s, 1, middle)
        for face in (0, 1):
            make_share(s, face)
        inside(s, middle, planes - 1)
        if s + 1 == SECTIONS:
            stores[0].start()
        for face in (0, 1):
            make_ghost(s, face)
            if face == 0:
                update(s, 0, lambda m: ghost[0, m], lambda m: src[m, 1])
            else:
                update(s, planes - 1, lambda m: src[m, planes - 2], lambda m: ghost[1, m])
            if s + 1 < SECTIONS:
                send_face(s + 1, 1 - face)
            else:
                stores[1 + face].start()

    for store in stores:
        store.wait()
    for k in (0, 1):
        donor_copy(k).wait_send()
    for s in range(SECTIONS):
        for side in (0, 1):
            halo_copy(s, side).wait_send()
        for face in (0, 1):
            @pl.when(has[1 - face])
            def _():
                for d in order:
                    face_copy(s, face, d).wait_send()

            @pl.when(has[face])
            def _():
                share_copy(s, face).wait_send()


def local(flow_state, velocity, offsets, passage_shift, donor_step, donor_weight):
    rows, count = lax.axis_size("row"), lax.axis_size("circ")
    comps, planes, radial, cells = flow_state.shape
    assert cells == LANES and 2 * planes * (radial // GROUP) == LANES
    whole = pl.BlockSpec(memory_space=pl.ANY)
    half = count // 2
    face = (comps, radial, cells)
    return pl.pallas_call(
        functools.partial(kernel, rows, count),
        out_shape=jax.ShapeDtypeStruct(flow_state.shape, flow_state.dtype),
        in_specs=[whole] * 6,
        out_specs=whole,
        scratch_shapes=[
            pltpu.VMEM(flow_state.shape, jnp.float32),
            pltpu.VMEM(velocity.shape, jnp.float32),
            pltpu.SMEM(offsets.shape, jnp.int32),
            pltpu.SMEM(passage_shift.shape, jnp.int32),
            pltpu.VMEM(donor_step.shape, jnp.int32),
            pltpu.VMEM(donor_weight.shape, jnp.float32),
            pltpu.VMEM(flow_state.shape, jnp.float32),
            pltpu.VMEM(flow_state.shape, jnp.float32),
            pltpu.VMEM(flow_state.shape, jnp.float32),
            pltpu.VMEM((SECTIONS, comps, GROUP, cells), jnp.float32),
            pltpu.VMEM((SECTIONS, 2, comps, GROUP, cells), jnp.float32),
            pltpu.VMEM((comps, GROUP, cells), jnp.float32),
            pltpu.VMEM((2, 2 * cells, 4 * cells), jnp.bfloat16),
            pltpu.VMEM((2, *face), jnp.float32),
            pltpu.VMEM((SECTIONS, 2, *face), jnp.float32),
            pltpu.VMEM((SECTIONS, 2, *face), jnp.float32),
            pltpu.VMEM(donor_step.shape, jnp.int32),
            pltpu.VMEM(donor_weight.shape, jnp.float32),
            pltpu.SemaphoreType.DMA((SECTIONS, 2, half)),
            pltpu.SemaphoreType.DMA((SECTIONS, 2, half)),
            pltpu.SemaphoreType.DMA((SECTIONS, 2)),
            pltpu.SemaphoreType.DMA((SECTIONS, 2)),
            pltpu.SemaphoreType.DMA((SECTIONS, 2)),
            pltpu.SemaphoreType.DMA((SECTIONS, 2)),
            pltpu.SemaphoreType.DMA((6,)),
            pltpu.SemaphoreType.DMA((3,)),
            pltpu.SemaphoreType.DMA((2,)),
            pltpu.SemaphoreType.DMA((2,)),
        ]
        + [pltpu.VMEM((half, *face), jnp.float32)] * (2 * SECTIONS),
        compiler_params=pltpu.CompilerParams(
            collective_id=0, has_side_effects=True, vmem_limit_bytes=63 * 1024 * 1024
        ),
    )(flow_state, velocity, offsets, passage_shift, donor_step, donor_weight)


def solution(mesh):
    placed = (
        P(None, "row", None, "circ"),
        P(None, "row", None, "circ"),
        P(),
        P(),
        P("row", None, "circ"),
        P("row", None, "circ"),
    )
    return jax.shard_map(
        local, mesh=mesh, in_specs=placed, out_specs=P(None, "row", None, "circ"), check_vma=False
    )
```
